512 devices in a mesh: col: 128 (over z, y, core), lev: 4 (over x).
Axes of the slice: x: 4, y: 8, z: 8, core: 2. Of those that a mesh axis runs over, the one named last changes fastest.
Arguments:
- state: bfloat16 [10, 128, 65536], P(None, 'lev', 'col'), may hold values from -6 to 6
- level_coupling: bfloat16 [10, 128, 128], replicated, may hold values from -0.5 to 0.5
- gwd_in: bfloat16 [1280, 512], replicated, may hold values from -0.15625 to 0.15625
- gwd_out: bfloat16 [512, 256], replicated, may hold values from -0.25 to 0.25
- sw_in: bfloat16 [1280, 512], replicated, may hold values from -0.15625 to 0.15625
- sw_out: bfloat16 [512, 128], replicated, may hold values from -0.25 to 0.25
- phys_device: int32 [16384], P('col'), may hold values from 0 to 127, as said below
- sunlit: int32 [16384], P('col'), may hold values from 0 to 1, as said below
Outputs:
- tendency: bfloat16 [10, 128, 65536], P(None, 'lev', 'col')
- sunlit_heating: bfloat16 [128, 32768], P(None, ('col', 'lev'))
The draws below stay inside these ranges and needn't reach their ends.
Inputs may be any that keep to these rules, and one draw needn't show every extreme that they name: The sunlit blocks form one cyclic run of half of the 16384 blocks in global order. `phys_device`: the 128 blocks of one dynamics device (blocks d * 128 to d * 128 + 127) go to 128 different physics devices, and every physics device receives exactly 64 sunlit blocks.
All inputs are finite; a program needn't handle non-finite values.
Results may differ from the reference program's by a relative error of at most 0.0045.
Values may be sent and summed in bfloat16 or wider, within the bound.
No kernel may reach another device: no remote copies, remote signals or barrier semaphores. Data moves between devices by JAX's collectives and lax.ppermute only.
A program may use at most 64 MiB of HBM per device.

```python
import jax
import jax.numpy as jnp
from jax import lax

FIELDS = 10
LEVELS = 128
NEURONS = 512
BLOCK = 4
BLOCKS_DEV = 128
BLOCKS = 16384
COLUMNS = 65536
SUN_COLS = 32768
N_COL = 128
N_LEV = 4


def day_side(key):
    offset = jax.random.randint(key, (), 0, BLOCKS)
    places = jnp.arange(BLOCKS, dtype=jnp.int32)
    return ((places - offset) % BLOCKS < BLOCKS // 2).astype(jnp.int32)


def draw_sunlit(key, part):
    return day_side(key)


def draw_phys_device(key, part):
    lit_grid = day_side(key).reshape(N_COL, BLOCKS_DEV)
    counts = jnp.sum(lit_grid, axis=1)
    before = jnp.cumsum(counts) - counts
    lit_rank = jnp.cumsum(lit_grid, axis=1) - 1
    dark_rank = counts[:, None] + jnp.cumsum(1 - lit_grid, axis=1) - 1
    within = jnp.where(lit_grid == 1, lit_rank, dark_rank)
    return ((before[:, None] + within) % BLOCKS_DEV).astype(jnp.int32).reshape(BLOCKS)


def steps_of(stream_key, extent, split, low, top_value):
    def one(dim, shards_of):
        heights = jax.random.uniform(jax.random.fold_in(jax.random.fold_in(stream_key, 6), dim), (shards_of,), jnp.float32, low / len(split), top_value / len(split))
        return jnp.repeat(jnp.exp(heights), extent[dim] // shards_of).reshape((-1,) + (1,) * (len(extent) - dim - 1))

    gain = one(*split[0])
    for cut in split[1:]:
        gain = gain * one(*cut)
    return gain


def bell_draw(rng, shape, width, reach, split=(), held_as=jnp.bfloat16):
    loudness = steps_of(rng, shape, split, -0.22, 0.18) if split else 1.0
    entries = jax.random.normal(rng, shape, jnp.float32) * width * loudness
    return jnp.minimum(jnp.maximum(entries, -reach), reach).astype(held_as)


def setup_inputs(seed: int = 0) -> dict:
    key_list = jax.random.split(jax.random.key(seed), 9)
    state = bell_draw(key_list[0], (FIELDS, LEVELS, COLUMNS), 1.0, 6.0, ((1, 4), (2, 128)))
    level_coupling = bell_draw(key_list[1], (FIELDS, LEVELS, LEVELS), LEVELS ** -0.5, 0.5)
    gwd_in = bell_draw(key_list[2], (FIELDS * LEVELS, NEURONS), (FIELDS * LEVELS) ** -0.5, 0.15625)
    gwd_out = bell_draw(key_list[3], (NEURONS, 2 * LEVELS), NEURONS ** -0.5, 0.25)
    sw_in = bell_draw(key_list[4], (FIELDS * LEVELS, NEURONS), (FIELDS * LEVELS) ** -0.5, 0.15625)
    sw_out = bell_draw(key_list[5], (NEURONS, LEVELS), NEURONS ** -0.5, 0.25)
    phys_device = draw_phys_device(jax.random.fold_in(key_list[8], 71), 0)
    sunlit = draw_sunlit(jax.random.fold_in(key_list[8], 71), 0)
    return dict(state=state, level_coupling=level_coupling, gwd_in=gwd_in, gwd_out=gwd_out, sw_in=sw_in, sw_out=sw_out, phys_device=phys_device, sunlit=sunlit)


def column_physics(column_state, level_coupling, gwd_in, gwd_out, sw_in, sw_out, lit_cols):
    fields, levels, count = column_state.shape
    stacked = column_state.reshape(fields * levels, count)
    coupled = jnp.einsum("fij,fjn->fin", level_coupling.astype(jnp.float32), column_state.astype(jnp.float32))
    drag_hidden = jnp.tanh(jnp.dot(gwd_in.T, stacked, preferred_element_type=jnp.float32)).astype(jnp.bfloat16)
    drag_rows = jnp.dot(gwd_out.T, drag_hidden, preferred_element_type=jnp.float32).reshape(2, levels, count)
    sw_hidden = jnp.tanh(jnp.dot(sw_in.T, stacked, preferred_element_type=jnp.float32)).astype(jnp.bfloat16)
    heating = jnp.dot(sw_out.T, sw_hidden, preferred_element_type=jnp.float32) * lit_cols[None, :]
    additions = jnp.concatenate([drag_rows, heating[None], jnp.zeros((fields - 3, levels, count), jnp.float32)], axis=0)
    return (coupled + additions).astype(jnp.bfloat16), heating


def reference(state, level_coupling, gwd_in, gwd_out, sw_in, sw_out, phys_device, sunlit):
    dev_cols = BLOCKS_DEV * BLOCK
    stacked = state.reshape(FIELDS, LEVELS, N_COL, dev_cols).transpose(2, 0, 1, 3)
    sun_cols = jnp.repeat(sunlit.astype(jnp.float32), BLOCK).reshape(N_COL, dev_cols)

    def device_work(operand):
        return column_physics(operand[0], level_coupling, gwd_in, gwd_out, sw_in, sw_out, operand[1])

    tend_all, heat_all = lax.map(device_work, (stacked, sun_cols))
    tendency = tend_all.transpose(1, 2, 0, 3).reshape(FIELDS, LEVELS, COLUMNS)
    heat_blocks = heat_all.transpose(1, 0, 2).reshape(LEVELS, BLOCKS, BLOCK)
    source = jnp.arange(BLOCKS, dtype=jnp.int32) // BLOCKS_DEV
    sort_keys = jnp.where(sunlit == 1, phys_device * BLOCKS_DEV + source, BLOCKS + BLOCKS).astype(jnp.int32)
    picked = jnp.argsort(sort_keys, stable=True)[: BLOCKS // 2]
    chosen = jnp.take(heat_blocks, picked, axis=1)
    quarter = BLOCK // N_LEV
    arranged = chosen.reshape(LEVELS, N_COL, BLOCKS_DEV // 2, N_LEV, quarter).transpose(0, 1, 3, 2, 4)
    arranged = arranged.reshape(LEVELS, SUN_COLS)
    return tendency, arranged.astype(jnp.bfloat16)
```

```python
import functools

import jax
import jax.numpy as jnp
from jax import lax
from jax.experimental import pallas as pl
from jax.experimental.pallas import tpu as pltpu
from jax.sharding import PartitionSpec as P

F32 = jnp.float32
BF16 = jnp.bfloat16
DARK = 2.0**100
GROUP = 4
WIDE = 384


def matmul(a, b, contract=((1,), (0,))):
    return lax.dot_general(a, b, (contract, ((), ())), preferred_element_type=F32)


def iota(shape, dim):
    return lax.broadcasted_iota(jnp.int32, shape, dim)


def onehot(mask):
    return jnp.where(mask, 1.0, 0.0).astype(BF16)


def per_column(row, blocks, block_cols):
    cols = blocks * block_cols
    spread = onehot(iota((blocks, cols), 1) // block_cols == iota((blocks, cols), 0))
    rows = jnp.broadcast_to(row.astype(F32), (16, blocks)).astype(BF16)
    return matmul(rows, spread)


def pack_kernel(state_ref, phys_ref, lit_ref, out_ref):
    rows, cols = state_ref.shape
    blocks = phys_ref.shape[1]
    block_cols = cols // blocks
    slots = blocks // GROUP
    dest = per_column(phys_ref[...], blocks, block_cols)[0:1].astype(jnp.int32)
    lit = per_column(lit_ref[...], blocks, block_cols)[0:1]
    place = ((dest % GROUP) * block_cols + iota((1, cols), 1) % block_cols) * slots + dest // GROUP
    sort = onehot(iota((cols, cols), 0) == place)
    flags = jnp.broadcast_to(lit, (WIDE - rows, cols)).astype(BF16)
    data = jnp.concatenate([state_ref[...], flags], axis=0)
    out_ref[...] = matmul(sort, data, ((1,), (1,))).astype(BF16)


def heat_kernel(got_ref, win_ref, wout_ref, out_ref):
    pieces, slots, _ = got_ref.shape
    levs = pieces // GROUP
    fields, levels, neurons = win_ref.shape
    part = levels // levs
    count = GROUP * slots
    total = None
    for lev in range(levs):
        cols = jnp.concatenate([got_ref[g * levs + lev] for g in range(GROUP)], axis=0)
        weight = win_ref[:, lev * part : (lev + 1) * part, :].reshape(fields * part, neurons)
        term = matmul(cols[:, : fields * part], weight)
        total = term if total is None else total + term
    lit = cols[:, fields * part : fields * part + 1].astype(F32)
    heat = matmul(jnp.tanh(total).astype(BF16), wout_ref[...])
    sent = jnp.where(lit > 0.5, heat, DARK).astype(BF16)
    row = iota((count, count), 0)
    order = onehot(iota((count, count), 1) == (row % GROUP) * slots + row // GROUP)
    out_ref[...] = matmul(order, sent).astype(BF16)


def pick_kernel(got_ref, out_ref):
    sources, levels = got_ref.shape
    picks = out_ref.shape[0]
    got = got_ref[...].astype(F32)
    lit = got < 0.5 * DARK
    heat = jnp.where(lit, got, 0.0).astype(BF16)
    lit_col = jnp.where(lit[:, :1], 1.0, 0.0)
    below = onehot(iota((sources, sources), 1) < iota((sources, sources), 0))
    rank = matmul(below, jnp.broadcast_to(lit_col, (sources, picks)).astype(BF16))
    choose = jnp.where(rank == iota((sources, picks), 1).astype(F32), lit_col, 0.0).astype(BF16)
    out_ref[...] = matmul(choose, heat, ((0,), (0,))).astype(BF16)


def tendency_kernel(
    lev_ref, x0, x1, x2, x3, coupling_ref, gin_ref, gout_ref, sin_ref, sout_ref, lit_ref, out_ref,
    whole, rows_ref,
):
    fields, part, cols = x0.shape
    levs = 4
    levels = part * levs
    blocks = lit_ref.shape[1]
    lev = lev_ref[0]
    for step, shard in enumerate((x0, x1, x2, x3)):
        source = lax.rem(lev + levs - step, levs)
        whole[:, pl.ds(pl.multiple_of(source * part, part), part), :] = shard[...]
    flat = whole[...].reshape(fields * levels, cols)
    hidden = jnp.tanh(matmul(flat, gin_ref[...], ((0,), (0,)))).astype(BF16)
    rows_ref[: 2 * levels] = matmul(gout_ref[...], hidden, ((0,), (1,)))
    hidden = jnp.tanh(matmul(flat, sin_ref[...], ((0,), (0,)))).astype(BF16)
    lit = per_column(lit_ref[...], blocks, cols // blocks)[0:1]
    rows_ref[2 * levels :] = matmul(sout_ref[...], hidden, ((0,), (1,))) * lit
    own = pl.multiple_of(lev * part, part)
    for field in range(fields):
        term = matmul(coupling_ref[field, pl.ds(own, part), :], whole[field])
        if field < 3:
            term = term + rows_ref[pl.ds(field * levels + own, part), :]
        out_ref[field] = term.astype(BF16)


def call(kernel, out, cost, scratch=(), smem=0, vmem=None, n_in=0):
    specs = [pl.BlockSpec(memory_space=pltpu.SMEM)] * smem
    specs += [pl.BlockSpec(memory_space=pltpu.VMEM)] * (n_in - smem)
    return pl.pallas_call(
        kernel,
        out_shape=jax.ShapeDtypeStruct(*out),
        in_specs=specs,
        out_specs=pl.BlockSpec(memory_space=pltpu.VMEM),
        scratch_shapes=list(scratch),
        cost_estimate=pl.CostEstimate(flops=cost[0], bytes_accessed=cost[1], transcendentals=0),
        compiler_params=pltpu.CompilerParams(vmem_limit_bytes=vmem or (24 << 20)),
    )


def local(state, level_coupling, gwd_in, gwd_out, sw_in, sw_out, phys_device, sunlit):
    fields, part, cols = state.shape
    blocks = phys_device.shape[0]
    levs = lax.axis_size("lev")
    col_count = lax.axis_size("col")
    levels = part * levs
    slots = blocks // GROUP
    members = GROUP * levs
    phys_row = phys_device.reshape(1, blocks)
    lit_row = sunlit.reshape(1, blocks)

    packed = call(pack_kernel, ((cols, WIDE), BF16), (2 * cols * cols * WIDE, 1 << 20), n_in=3)(
        state.reshape(fields * part, cols), phys_row, lit_row
    ).reshape(members, slots, WIDE)
    near = [[e * members + i for i in range(members)] for e in range(col_count // GROUP)]
    got = lax.all_to_all(packed, ("col", "lev"), 0, 0, tiled=True, axis_index_groups=near)

    shards = [state] + [
        lax.ppermute(state, "lev", [(i, (i + k) % levs) for i in range(levs)]) for k in (1, 2, 3)
    ]

    heat = call(
        heat_kernel, ((slots * GROUP, levels), BF16),
        (2 * blocks * (fields * levels * 512 + 512 * levels), 2 << 20), n_in=3,
    )(got, sw_in.reshape(fields, levels, -1), sw_out)
    far = [[e * GROUP + g for e in range(col_count // GROUP)] for g in range(GROUP)]
    arrived = lax.all_to_all(
        heat.reshape(slots, GROUP, levels), "col", 0, 0, tiled=True, axis_index_groups=far
    ).reshape(col_count, levels)

    lev = lax.axis_index("lev").astype(jnp.int32).reshape(1)
    tendency = call(
        tendency_kernel, ((fields, part, cols), BF16),
        (2 * cols * (fields * levels * 1024 + 512 * 3 * levels), 5 << 20),
        scratch=[pltpu.VMEM((fields, levels, cols), BF16), pltpu.VMEM((3 * levels, cols), F32)],
        smem=1, n_in=11,
    )(lev, *shards, level_coupling, gwd_in, gwd_out, sw_in, sw_out, lit_row)

    picked = call(pick_kernel, ((blocks // 2, levels), BF16), (1 << 22, 1 << 16), n_in=1)(arrived)
    return tendency, picked.T


def solution(mesh):
    return jax.shard_map(
        local,
        mesh=mesh,
        in_specs=(P(None, "lev", "col"), P(), P(), P(), P(), P(), P("col"), P("col")),
        out_specs=(P(None, "lev", "col"), P(None, ("col", "lev"))),
        check_vma=False,
    )
```

```python
import jax
import jax.numpy as jnp
from jax import lax
from jax.experimental import pallas as pl
from jax.experimental.pallas import tpu as pltpu
from jax.sharding import PartitionSpec as P

F32 = jnp.float32
BF16 = jnp.bfloat16
DARK = 2.0**100
GROUP = 4
WIDE = 384
PIECES = 2


def matmul(a, b, contract=((1,), (0,))):
    return lax.dot_general(a, b, (contract, ((), ())), preferred_element_type=F32)


def iota(shape, dim):
    return lax.broadcasted_iota(jnp.int32, shape, dim)


def onehot(mask):
    return jnp.where(mask, 1.0, 0.0).astype(BF16)


def per_column(row, blocks, block_cols):
    cols = blocks * block_cols
    spread = onehot(iota((blocks, cols), 1) // block_cols == iota((blocks, cols), 0))
    rows = jnp.broadcast_to(row.astype(F32), (16, blocks)).astype(BF16)
    return matmul(rows, spread)


def pack_kernel(state_hbm, phys_hbm, lit_hbm, out_hbm, data, phys_row, lit_row, packed, sems):
    fields, part, cols = state_hbm.shape
    blocks = phys_row.shape[1]
    block_cols = cols // blocks
    slots = blocks // GROUP
    copies = [
        pltpu.make_async_copy(phys_hbm, phys_row, sems.at[0]),
        pltpu.make_async_copy(lit_hbm, lit_row, sems.at[1]),
        pltpu.make_async_copy(state_hbm, data.at[:fields], sems.at[2]),
    ]
    for copy in copies:
        copy.start()
    spread = onehot(iota((blocks, cols), 1) // block_cols == iota((blocks, cols), 0))
    column = iota((1, cols), 1) % block_cols
    copies[0].wait()
    copies[1].wait()
    both = jnp.where(iota((16, blocks), 0) == 0, phys_row[...], lit_row[...])
    both = matmul(both.astype(F32).astype(BF16), spread)
    dest = both[0:1].astype(jnp.int32)
    place = ((dest % GROUP) * block_cols + column) * slots + dest // GROUP
    data[fields:] = jnp.broadcast_to(both[1:2], (2, part, cols)).astype(BF16)
    piece = cols // PIECES
    sorts = [onehot(iota((piece, cols), 0) + c * piece == place) for c in range(PIECES)]
    copies[2].wait()
    flat = data[...].reshape(WIDE, cols)
    writes = []
    for c, sort in enumerate(sorts):
        rows_c = pl.ds(c * piece, piece)
        packed[rows_c] = matmul(sort, flat, ((1,), (1,))).astype(BF16)
        writes.append(pltpu.make_async_copy(packed.at[rows_c], out_hbm.at[rows_c], sems.at[3 + c]))
        writes[-1].start()
    for write in writes:
        write.wait()


def heat_kernel(got_ref, win_ref, wout_ref, out_ref):
    pieces, slots, _ = got_ref.shape
    levs = pieces // GROUP
    fields, levels, neurons = win_ref.shape
    part = levels // levs
    count = GROUP * slots
    total = None
    for lev in range(levs):
        cols = jnp.concatenate([got_ref[g * levs + lev] for g in range(GROUP)], axis=0)
        weight = win_ref[:, lev * part : (lev + 1) * part, :].reshape(fields * part, neurons)
        term = matmul(cols[:, : fields * part], weight)
        total = term if total is None else total + term
    lit = cols[:, fields * part : fields * part + 1].astype(F32)
    heat = matmul(jnp.tanh(total).astype(BF16), wout_ref[...])
    sent = jnp.where(lit > 0.5, heat, DARK).astype(BF16)
    row = iota((count, count), 0)
    order = onehot(iota((count, count), 1) == (row % GROUP) * slots + row // GROUP)
    out_ref[...] = matmul(order, sent).astype(BF16)


def pick_kernel(got_ref, out_ref):
    sources, levels = got_ref.shape
    picks = out_ref.shape[0]
    got = got_ref[...].astype(F32)
    lit = got < 0.5 * DARK
    heat = jnp.where(lit, got, 0.0).astype(BF16)
    lit_col = jnp.where(lit[:, :1], 1.0, 0.0)
    below = onehot(iota((sources, sources), 1) < iota((sources, sources), 0))
    rank = matmul(below, jnp.broadcast_to(lit_col, (sources, picks)).astype(BF16))
    choose = jnp.where(rank == iota((sources, picks), 1).astype(F32), lit_col, 0.0).astype(BF16)
    out_ref[...] = matmul(choose, heat, ((0,), (0,))).astype(BF16)


def tendency_kernel(
    lev_ref, x0, x1, x2, x3, coupling_hbm, gin_hbm, gout_hbm, sin_hbm, sout_hbm, lit_hbm, out_hbm,
    whole, coupling, gin, gout, sin, sout, lit_row, terms, drag, out, sems,
):
    fields, levels, cols = whole.shape
    part = out.shape[1]
    levs = levels // part
    blocks = lit_row.shape[1]
    lev = lev_ref[0]
    copies = []
    for step, shard in enumerate((x0, x1, x2, x3)):
        source = pl.multiple_of((lev ^ step) * part, part)
        copies.append(
            pltpu.make_async_copy(shard, whole.at[:, pl.ds(source, part), :], sems.at[step])
        )
    for source, target in (
        (coupling_hbm, coupling), (gin_hbm, gin), (gout_hbm, gout),
        (sin_hbm, sin), (sout_hbm, sout), (lit_hbm, lit_row),
    ):
        copies.append(pltpu.make_async_copy(source, target, sems.at[len(copies)]))
    for copy in copies:
        copy.start()
    own = pl.multiple_of(lev * part, part)
    for copy in copies[: levs + 1]:
        copy.wait()
    for field in range(fields):
        term = matmul(coupling[field, pl.ds(own, part), :], whole[field])
        if field < 3:
            terms[field] = term
        else:
            out[field] = term.astype(BF16)
    first = pltpu.make_async_copy(out.at[3:], out_hbm.at[3:], sems.at[len(copies)])
    first.start()
    flat = whole[...].reshape(fields * levels, cols)
    copies[levs + 1].wait()
    hidden = jnp.tanh(matmul(flat, gin[...], ((0,), (0,)))).astype(BF16)
    copies[levs + 2].wait()
    drag[: 2 * levels] = matmul(gout[...], hidden, ((0,), (1,)))
    copies[levs + 3].wait()
    hidden = jnp.tanh(matmul(flat, sin[...], ((0,), (0,)))).astype(BF16)
    copies[levs + 4].wait()
    copies[levs + 5].wait()
    lit = per_column(lit_row[...], blocks, cols // blocks)[0:1]
    drag[2 * levels :] = matmul(sout[...], hidden, ((0,), (1,))) * lit
    for field in range(3):
        added = drag[pl.ds(field * levels + own, part), :]
        out[field] = (terms[field] + added).astype(BF16)
    last = pltpu.make_async_copy(out.at[:3], out_hbm.at[:3], sems.at[len(copies) + 1])
    last.start()
    first.wait()
    last.wait()


def call(kernel, out, cost, spaces, scratch=(), vmem=24, result="v"):
    kinds = {"s": pltpu.SMEM, "v": pltpu.VMEM, "h": pltpu.HBM}
    return pl.pallas_call(
        kernel,
        out_shape=jax.ShapeDtypeStruct(*out),
        in_specs=[pl.BlockSpec(memory_space=kinds[space]) for space in spaces],
        out_specs=pl.BlockSpec(memory_space=kinds[result]),
        scratch_shapes=list(scratch),
        cost_estimate=pl.CostEstimate(flops=cost[0], bytes_accessed=cost[1], transcendentals=0),
        compiler_params=pltpu.CompilerParams(vmem_limit_bytes=vmem << 20),
    )


def local(state, level_coupling, gwd_in, gwd_out, sw_in, sw_out, phys_device, sunlit):
    fields, part, cols = state.shape
    blocks = phys_device.shape[0]
    levs = lax.axis_size("lev")
    col_count = lax.axis_size("col")
    levels = part * levs
    slots = blocks // GROUP
    members = GROUP * levs
    phys_row = phys_device.reshape(1, blocks)
    lit_row = sunlit.reshape(1, blocks)

    packed = call(
        pack_kernel, ((cols, WIDE), BF16), (2 * cols * cols * WIDE, 1 << 20), "hhh",
        [
            pltpu.VMEM((fields + 2, part, cols), BF16),
            pltpu.VMEM((1, blocks), jnp.int32),
            pltpu.VMEM((1, blocks), jnp.int32),
            pltpu.VMEM((cols, WIDE), BF16),
            pltpu.SemaphoreType.DMA((3 + PIECES,)),
        ],
        62, "h",
    )(state, phys_row, lit_row).reshape(members, slots, WIDE)
    near = [[e * members + i for i in range(members)] for e in range(col_count // GROUP)]
    got = lax.all_to_all(packed, ("col", "lev"), 0, 0, tiled=True, axis_index_groups=near)

    ring = [[(i, i ^ step) for i in range(levs)] for step in range(levs)]
    shards = [state] + [lax.ppermute(state, "lev", ring[step]) for step in range(1, levs)]

    heat = call(
        heat_kernel, ((slots * GROUP, levels), BF16),
        (2 * blocks * (fields * levels * 512 + 512 * levels), 2 << 20), "vvv",
    )(got, sw_in.reshape(fields, levels, -1), sw_out)
    far = [[e * GROUP + g for e in range(col_count // GROUP)] for g in range(GROUP)]
    arrived = lax.all_to_all(
        heat.reshape(slots, GROUP, levels), "col", 0, 0, tiled=True, axis_index_groups=far
    ).reshape(col_count, levels)

    lev = lax.axis_index("lev").astype(jnp.int32).reshape(1)
    tendency = call(
        tendency_kernel, ((fields, part, cols), BF16),
        (2 * cols * (fields * levels * 1024 + 512 * 3 * levels), 5 << 20), "s" + "h" * 10,
        [
            pltpu.VMEM((fields, levels, cols), BF16),
            pltpu.VMEM(level_coupling.shape, BF16),
            pltpu.VMEM(gwd_in.shape, BF16),
            pltpu.VMEM(gwd_out.shape, BF16),
            pltpu.VMEM(sw_in.shape, BF16),
            pltpu.VMEM(sw_out.shape, BF16),
            pltpu.VMEM((1, blocks), jnp.int32),
            pltpu.VMEM((3, part, cols), F32),
            pltpu.VMEM((3 * levels, cols), F32),
            pltpu.VMEM((fields, part, cols), BF16),
            pltpu.SemaphoreType.DMA((levs + 8,)),
        ],
        63, "h",
    )(lev, *shards, level_coupling, gwd_in, gwd_out, sw_in, sw_out, lit_row)

    picked = call(pick_kernel, ((blocks // 2, levels), BF16), (1 << 22, 1 << 16), "v")(arrived)
    return tendency, picked.T


def solution(mesh):
    return jax.shard_map(
        local,
        mesh=mesh,
        in_specs=(P(None, "lev", "col"), P(), P(), P(), P(), P(), P("col"), P("col")),
        out_specs=(P(None, "lev", "col"), P(None, ("col", "lev"))),
        check_vma=False,
    )
```

```python
import jax
import jax.numpy as jnp
from jax import lax
from jax.experimental import pallas as pl
from jax.experimental.pallas import tpu as pltpu
from jax.sharding import PartitionSpec as P

F32 = jnp.float32
BF16 = jnp.bfloat16
DARK = 2.0**100
GROUP = 4
WIDE = 384
PIECES = 2
HEAD = 22


def matmul(a, b, contract=((1,), (0,))):
    return lax.dot_general(a, b, (contract, ((), ())), preferred_element_type=F32)


def iota(shape, dim):
    return lax.broadcasted_iota(jnp.int32, shape, dim)


def onehot(mask):
    return jnp.where(mask, 1.0, 0.0).astype(BF16)


def per_column(row, blocks, block_cols):
    cols = blocks * block_cols
    spread = onehot(iota((blocks, cols), 1) // block_cols == iota((blocks, cols), 0))
    rows = jnp.broadcast_to(row.astype(F32), (16, blocks)).astype(BF16)
    return matmul(rows, spread)


def pack_kernel(state_hbm, phys_hbm, lit_hbm, out_hbm, data, phys_row, lit_row, packed, sems):
    fields, part, cols = state_hbm.shape
    blocks = phys_row.shape[1]
    block_cols = cols // blocks
    slots = blocks // GROUP
    copies = [
        pltpu.make_async_copy(phys_hbm, phys_row, sems.at[0]),
        pltpu.make_async_copy(lit_hbm, lit_row, sems.at[1]),
        pltpu.make_async_copy(state_hbm, data.at[:fields], sems.at[2]),
    ]
    for copy in copies:
        copy.start()
    spread = onehot(iota((blocks, cols), 1) // block_cols == iota((blocks, cols), 0))
    column = iota((1, cols), 1) % block_cols
    copies[0].wait()
    copies[1].wait()
    both = jnp.where(iota((16, blocks), 0) == 0, phys_row[...], lit_row[...])
    both = matmul(both.astype(F32).astype(BF16), spread)
    dest = both[0:1].astype(jnp.int32)
    place = ((dest % GROUP) * block_cols + column) * slots + dest // GROUP
    data[fields:] = jnp.broadcast_to(both[1:2], (2, part, cols)).astype(BF16)
    piece = cols // PIECES
    sorts = [onehot(iota((piece, cols), 0) + c * piece == place) for c in range(PIECES)]
    copies[2].wait()
    flat = data[...].reshape(WIDE, cols)
    writes = []
    for c, sort in enumerate(sorts):
        rows_c = pl.ds(c * piece, piece)
        packed[rows_c] = matmul(sort, flat, ((1,), (1,))).astype(BF16)
        writes.append(pltpu.make_async_copy(packed.at[rows_c], out_hbm.at[rows_c], sems.at[3 + c]))
        writes[-1].start()
    for write in writes:
        write.wait()


def heat_kernel(got_ref, win_ref, wout_ref, out_ref):
    pieces, slots, _ = got_ref.shape
    levs = pieces // GROUP
    fields, levels, neurons = win_ref.shape
    part = levels // levs
    count = GROUP * slots
    total = None
    for lev in range(levs):
        cols = jnp.concatenate([got_ref[g * levs + lev] for g in range(GROUP)], axis=0)
        weight = win_ref[:, lev * part : (lev + 1) * part, :].reshape(fields * part, neurons)
        term = matmul(cols[:, : fields * part], weight)
        total = term if total is None else total + term
    lit = cols[:, fields * part : fields * part + 1].astype(F32)
    heat = matmul(jnp.tanh(total).astype(BF16), wout_ref[...])
    sent = jnp.where(lit > 0.5, heat, DARK).astype(BF16)
    row = iota((count, count), 0)
    slot = (row // GROUP + HEAD) % slots
    order = onehot(iota((count, count), 1) == (row % GROUP) * slots + slot)
    out_ref[...] = matmul(order, sent).astype(BF16)


def pick_kernel(got_ref, out_ref):
    sources, levels = got_ref.shape
    row, col = iota((sources, sources), 0), iota((sources, sources), 1)
    picks = out_ref.shape[0]
    got = got_ref[...].astype(F32)
    lit = got < 0.5 * DARK
    heat = jnp.where(lit, got, 0.0).astype(BF16)
    lit_col = jnp.where(lit[:, :1], 1.0, 0.0)
    turn = sources - HEAD * GROUP
    place = [jnp.where(i < turn, i + HEAD * GROUP, i - turn) for i in (row, col)]
    below = onehot(place[1] < place[0])
    rank = matmul(below, jnp.broadcast_to(lit_col, (sources, picks)).astype(BF16))
    choose = jnp.where(rank == iota((sources, picks), 1).astype(F32), lit_col, 0.0).astype(BF16)
    out_ref[...] = matmul(choose, heat, ((0,), (0,))).astype(BF16)


def tendency_kernel(
    lev_ref, x0, x1, x2, x3, coupling_hbm, gin_hbm, gout_hbm, sin_hbm, sout_hbm, lit_hbm, out_hbm,
    whole, coupling, gin, gout, sin, sout, lit_row, terms, drag, out, sems,
):
    fields, levels, cols = whole.shape
    part = out.shape[1]
    levs = levels // part
    blocks = lit_row.shape[1]
    lev = lev_ref[0]
    copies = []
    for step, shard in enumerate((x0, x1, x2, x3)):
        source = pl.multiple_of((lev ^ step) * part, part)
        copies.append(
            pltpu.make_async_copy(shard, whole.at[:, pl.ds(source, part), :], sems.at[step])
        )
    for source, target in (
        (coupling_hbm, coupling), (gin_hbm, gin), (gout_hbm, gout),
        (sin_hbm, sin), (sout_hbm, sout), (lit_hbm, lit_row),
    ):
        copies.append(pltpu.make_async_copy(source, target, sems.at[len(copies)]))
    for copy in copies:
        copy.start()
    own = pl.multiple_of(lev * part, part)
    for copy in copies[: levs + 1]:
        copy.wait()
    for field in range(fields):
        term = matmul(coupling[field, pl.ds(own, part), :], whole[field])
        if field < 3:
            terms[field] = term
        else:
            out[field] = term.astype(BF16)
    first = pltpu.make_async_copy(out.at[3:], out_hbm.at[3:], sems.at[len(copies)])
    first.start()
    flat = whole[...].reshape(fields * levels, cols)
    copies[levs + 1].wait()
    hidden = jnp.tanh(matmul(flat, gin[...], ((0,), (0,)))).astype(BF16)
    copies[levs + 2].wait()
    drag[: 2 * levels] = matmul(gout[...], hidden, ((0,), (1,)))
    copies[levs + 3].wait()
    hidden = jnp.tanh(matmul(flat, sin[...], ((0,), (0,)))).astype(BF16)
    copies[levs + 4].wait()
    copies[levs + 5].wait()
    lit = per_column(lit_row[...], blocks, cols // blocks)[0:1]
    drag[2 * levels :] = matmul(sout[...], hidden, ((0,), (1,))) * lit
    for field in range(3):
        added = drag[pl.ds(field * levels + own, part), :]
        out[field] = (terms[field] + added).astype(BF16)
    last = pltpu.make_async_copy(out.at[:3], out_hbm.at[:3], sems.at[len(copies) + 1])
    last.start()
    first.wait()
    last.wait()


def call(kernel, out, cost, spaces, scratch=(), vmem=24, result="v"):
    kinds = {"s": pltpu.SMEM, "v": pltpu.VMEM, "h": pltpu.HBM}
    return pl.pallas_call(
        kernel,
        out_shape=jax.ShapeDtypeStruct(*out),
        in_specs=[pl.BlockSpec(memory_space=kinds[space]) for space in spaces],
        out_specs=pl.BlockSpec(memory_space=kinds[result]),
        scratch_shapes=list(scratch),
        cost_estimate=pl.CostEstimate(flops=cost[0], bytes_accessed=cost[1], transcendentals=0),
        compiler_params=pltpu.CompilerParams(vmem_limit_bytes=vmem << 20),
    )


def local(state, level_coupling, gwd_in, gwd_out, sw_in, sw_out, phys_device, sunlit):
    fields, part, cols = state.shape
    blocks = phys_device.shape[0]
    levs = lax.axis_size("lev")
    col_count = lax.axis_size("col")
    levels = part * levs
    slots = blocks // GROUP
    members = GROUP * levs
    phys_row = phys_device.reshape(1, blocks)
    lit_row = sunlit.reshape(1, blocks)

    packed = call(
        pack_kernel, ((cols, WIDE), BF16), (2 * cols * cols * WIDE, 1 << 20), "hhh",
        [
            pltpu.VMEM((fields + 2, part, cols), BF16),
            pltpu.VMEM((1, blocks), jnp.int32),
            pltpu.VMEM((1, blocks), jnp.int32),
            pltpu.VMEM((cols, WIDE), BF16),
            pltpu.SemaphoreType.DMA((3 + PIECES,)),
        ],
        62, "h",
    )(state, phys_row, lit_row).reshape(members, slots, WIDE)
    near = [[e * members + i for i in range(members)] for e in range(col_count // GROUP)]
    got = lax.all_to_all(packed, ("col", "lev"), 0, 0, tiled=True, axis_index_groups=near)

    ring = [[(i, i ^ step) for i in range(levs)] for step in range(levs)]
    shards = [state] + [lax.ppermute(state, "lev", ring[step]) for step in range(1, levs)]

    heat = call(
        heat_kernel, ((slots * GROUP, levels), BF16),
        (2 * blocks * (fields * levels * 512 + 512 * levels), 2 << 20), "vvv",
    )(got, sw_in.reshape(fields, levels, -1), sw_out)
    far = [[(e + HEAD) % slots * GROUP + g for e in range(slots)] for g in range(GROUP)]
    arrived = lax.all_to_all(
        heat.reshape(slots, GROUP, levels), "col", 0, 0, tiled=True, axis_index_groups=far
    ).reshape(col_count, levels)

    lev = lax.axis_index("lev").astype(jnp.int32).reshape(1)
    tendency = call(
        tendency_kernel, ((fields, part, cols), BF16),
        (2 * cols * (fields * levels * 1024 + 512 * 3 * levels), 5 << 20), "s" + "h" * 10,
        [
            pltpu.VMEM((fields, levels, cols), BF16),
            pltpu.VMEM(level_coupling.shape, BF16),
            pltpu.VMEM(gwd_in.shape, BF16),
            pltpu.VMEM(gwd_out.shape, BF16),
            pltpu.VMEM(sw_in.shape, BF16),
            pltpu.VMEM(sw_out.shape, BF16),
            pltpu.VMEM((1, blocks), jnp.int32),
            pltpu.VMEM((3, part, cols), F32),
            pltpu.VMEM((3 * levels, cols), F32),
            pltpu.VMEM((fields, part, cols), BF16),
            pltpu.SemaphoreType.DMA((levs + 8,)),
        ],
        63, "h",
    )(lev, *shards, level_coupling, gwd_in, gwd_out, sw_in, sw_out, lit_row)

    picked = call(pick_kernel, ((blocks // 2, levels), BF16), (1 << 22, 1 << 16), "v")(arrived)
    return tendency, picked.T


def solution(mesh):
    return jax.shard_map(
        local,
        mesh=mesh,
        in_specs=(P(None, "lev", "col"), P(), P(), P(), P(), P(), P("col"), P("col")),
        out_specs=(P(None, "lev", "col"), P(None, ("col", "lev"))),
        check_vma=False,
    )
```

```python
import functools

import jax
import jax.numpy as jnp
from jax import lax
from jax.experimental import pallas as pl
from jax.experimental.pallas import tpu as pltpu
from jax.sharding import PartitionSpec as P

F32 = jnp.float32
BF16 = jnp.bfloat16
DARK = 2.0**100
GROUP = 4
WIDE = 384
PIECES = 2
HEAD = 26


def matmul(a, b, contract=((1,), (0,))):
    return lax.dot_general(a, b, (contract, ((), ())), preferred_element_type=F32)


def iota(shape, dim):
    return lax.broadcasted_iota(jnp.int32, shape, dim)


def onehot(mask):
    return jnp.where(mask, 1.0, 0.0).astype(BF16)


def per_column(row, blocks, block_cols):
    cols = blocks * block_cols
    spread = onehot(iota((blocks, cols), 1) // block_cols == iota((blocks, cols), 0))
    rows = jnp.broadcast_to(row.astype(F32), (16, blocks)).astype(BF16)
    return matmul(rows, spread)


def pack_kernel(state_hbm, phys_hbm, lit_hbm, out_hbm, data, phys_row, lit_row, packed, sems):
    fields, part, cols = state_hbm.shape
    blocks = phys_row.shape[1]
    block_cols = cols // blocks
    slots = blocks // GROUP
    copies = [
        pltpu.make_async_copy(phys_hbm, phys_row, sems.at[0]),
        pltpu.make_async_copy(lit_hbm, lit_row, sems.at[1]),
        pltpu.make_async_copy(state_hbm, data.at[:fields], sems.at[2]),
    ]
    for copy in copies:
        copy.start()
    spread = onehot(iota((blocks, cols), 1) // block_cols == iota((blocks, cols), 0))
    column = iota((1, cols), 1) % block_cols
    copies[0].wait()
    copies[1].wait()
    both = jnp.where(iota((16, blocks), 0) == 0, phys_row[...], lit_row[...])
    both = matmul(both.astype(F32).astype(BF16), spread)
    dest = both[0:1].astype(jnp.int32)
    place = ((dest % GROUP) * block_cols + column) * slots + dest // GROUP
    data[fields:] = jnp.broadcast_to(both[1:2], (2, part, cols)).astype(BF16)
    piece = cols // PIECES
    sorts = [onehot(iota((piece, cols), 0) + c * piece == place) for c in range(PIECES)]
    copies[2].wait()
    flat = data[...].reshape(WIDE, cols)
    writes = []
    for c, sort in enumerate(sorts):
        rows_c = pl.ds(c * piece, piece)
        packed[rows_c] = matmul(sort, flat, ((1,), (1,))).astype(BF16)
        writes.append(pltpu.make_async_copy(packed.at[rows_c], out_hbm.at[rows_c], sems.at[3 + c]))
        writes[-1].start()
    for write in writes:
        write.wait()


def heat_kernel(got_ref, win_ref, wout_ref, out_ref):
    pieces, slots, _ = got_ref.shape
    levs = pieces // GROUP
    fields, levels, neurons = win_ref.shape
    part = levels // levs
    count = GROUP * slots
    total = None
    for lev in range(levs):
        cols = jnp.concatenate([got_ref[g * levs + lev] for g in range(GROUP)], axis=0)
        weight = win_ref[:, lev * part : (lev + 1) * part, :].reshape(fields * part, neurons)
        term = matmul(cols[:, : fields * part], weight)
        total = term if total is None else total + term
    lit = cols[:, fields * part : fields * part + 1].astype(F32)
    heat = matmul(jnp.tanh(total).astype(BF16), wout_ref[...])
    sent = jnp.where(lit > 0.5, heat, DARK).astype(BF16)
    row = iota((count, count), 0)
    slot = (row // GROUP + HEAD) % slots
    order = onehot(iota((count, count), 1) == (row % GROUP) * slots + slot)
    out_ref[...] = matmul(order, sent).astype(BF16)


def pick_kernel(got_ref, out_ref):
    sources, levels = got_ref.shape
    row, col = iota((sources, sources), 0), iota((sources, sources), 1)
    picks = out_ref.shape[0]
    got = got_ref[...].astype(F32)
    lit = got < 0.5 * DARK
    heat = jnp.where(lit, got, 0.0).astype(BF16)
    lit_col = jnp.where(lit[:, :1], 1.0, 0.0)
    turn = sources - HEAD * GROUP
    place = [jnp.where(i < turn, i + HEAD * GROUP, i - turn) for i in (row, col)]
    below = onehot(place[1] < place[0])
    rank = matmul(below, jnp.broadcast_to(lit_col, (sources, picks)).astype(BF16))
    choose = jnp.where(rank == iota((sources, picks), 1).astype(F32), lit_col, 0.0).astype(BF16)
    out_ref[...] = matmul(choose, heat, ((0,), (0,))).astype(BF16)


def tendency_kernel(
    lev_ref, x0, x1, x2, x3, coupling_hbm, gin, gout_hbm, sin, sout, lit_hbm, out_hbm,
    whole, coupling, gout, lit_row, terms, drag, out, sems,
):
    fields, levels, cols = whole.shape
    part = out.shape[1]
    levs = levels // part
    blocks = lit_row.shape[1]
    lev = lev_ref[0]
    copies = []
    for step, shard in enumerate((x0, x1, x2, x3)):
        source = pl.multiple_of((lev ^ step) * part, part)
        copies.append(
            pltpu.make_async_copy(shard, whole.at[:, pl.ds(source, part), :], sems.at[step])
        )
    for source, target in (
        (coupling_hbm, coupling), (gout_hbm, gout), (lit_hbm, lit_row),
    ):
        copies.append(pltpu.make_async_copy(source, target, sems.at[len(copies)]))
    for copy in copies:
        copy.start()
    own = pl.multiple_of(lev * part, part)
    for copy in copies[: levs + 1]:
        copy.wait()
    for field in range(fields):
        term = matmul(coupling[field, pl.ds(own, part), :], whole[field])
        if field < 3:
            terms[field] = term
        else:
            out[field] = term.astype(BF16)
    first = pltpu.make_async_copy(out.at[3:], out_hbm.at[3:], sems.at[len(copies)])
    first.start()
    flat = whole[...].reshape(fields * levels, cols)
    hidden = jnp.tanh(matmul(flat, gin[...], ((0,), (0,)))).astype(BF16)
    copies[levs + 1].wait()
    drag[: 2 * levels] = matmul(gout[...], hidden, ((0,), (1,)))
    hidden = jnp.tanh(matmul(flat, sin[...], ((0,), (0,)))).astype(BF16)
    copies[levs + 2].wait()
    lit = per_column(lit_row[...], blocks, cols // blocks)[0:1]
    drag[2 * levels :] = matmul(sout[...], hidden, ((0,), (1,))) * lit
    for field in range(3):
        added = drag[pl.ds(field * levels + own, part), :]
        out[field] = (terms[field] + added).astype(BF16)
    last = pltpu.make_async_copy(out.at[:3], out_hbm.at[:3], sems.at[len(copies) + 1])
    last.start()
    first.wait()
    last.wait()


def call(kernel, out, cost, spaces, scratch=(), vmem=24, result="v"):
    kinds = {"s": pltpu.SMEM, "v": pltpu.VMEM, "h": pltpu.HBM}
    return pl.pallas_call(
        kernel,
        out_shape=jax.ShapeDtypeStruct(*out),
        in_specs=[pl.BlockSpec(memory_space=kinds[space]) for space in spaces],
        out_specs=pl.BlockSpec(memory_space=kinds[result]),
        scratch_shapes=list(scratch),
        cost_estimate=pl.CostEstimate(flops=cost[0], bytes_accessed=cost[1], transcendentals=0),
        compiler_params=pltpu.CompilerParams(vmem_limit_bytes=int(vmem * 1024) << 10),
    )


def local(state, level_coupling, gwd_in, gwd_out, sw_in, sw_out, phys_device, sunlit):
    fields, part, cols = state.shape
    blocks = phys_device.shape[0]
    levs = lax.axis_size("lev")
    col_count = lax.axis_size("col")
    levels = part * levs
    slots = blocks // GROUP
    members = GROUP * levs
    phys_row = phys_device.reshape(1, blocks)
    lit_row = sunlit.reshape(1, blocks)

    keep = functools.partial(pltpu.with_memory_space_constraint, memory_space=pltpu.HBM)
    packed = call(
        pack_kernel, ((cols, WIDE), BF16), (2 * cols * cols * WIDE, 1 << 20), "hhh",
        [
            pltpu.VMEM((fields + 2, part, cols), BF16),
            pltpu.VMEM((1, blocks), jnp.int32),
            pltpu.VMEM((1, blocks), jnp.int32),
            pltpu.VMEM((cols, WIDE), BF16),
            pltpu.SemaphoreType.DMA((3 + PIECES,)),
        ],
        24, "h",
    )(keep(state), keep(phys_row), keep(lit_row)).reshape(members, slots, WIDE)
    near = [[e * members + i for i in range(members)] for e in range(col_count // GROUP)]
    got = lax.all_to_all(packed, ("col", "lev"), 0, 0, tiled=True, axis_index_groups=near)

    ring = [[(i, i ^ step) for i in range(levs)] for step in range(levs)]
    shards = [state] + [lax.ppermute(state, "lev", ring[step]) for step in range(1, levs)]

    heat = call(
        heat_kernel, ((slots * GROUP, levels), BF16),
        (2 * blocks * (fields * levels * 512 + 512 * levels), 2 << 20), "vvv",
    )(got, sw_in.reshape(fields, levels, -1), sw_out)
    far = [[(e + HEAD) % slots * GROUP + g for e in range(slots)] for g in range(GROUP)]
    arrived = lax.all_to_all(
        heat.reshape(slots, GROUP, levels), "col", 0, 0, tiled=True, axis_index_groups=far
    ).reshape(col_count, levels)

    lev = lax.axis_index("lev").astype(jnp.int32).reshape(1)
    tendency = call(
        tendency_kernel, ((fields, part, cols), BF16),
        (2 * cols * (fields * levels * 1024 + 512 * 3 * levels), 5 << 20), "shhhhhvhvvh",
        [
            pltpu.VMEM((fields, levels, cols), BF16),
            pltpu.VMEM(level_coupling.shape, BF16),
            pltpu.VMEM(gwd_out.shape, BF16),
            pltpu.VMEM((1, blocks), jnp.int32),
            pltpu.VMEM((3, part, cols), F32),
            pltpu.VMEM((3 * levels, cols), F32),
            pltpu.VMEM((fields, part, cols), BF16),
            pltpu.SemaphoreType.DMA((levs + 8,)),
        ],
        40, "h",
    )(lev, *shards, keep(level_coupling), gwd_in, keep(gwd_out), sw_in, sw_out, keep(lit_row))

    picked = call(pick_kernel, ((blocks // 2, levels), BF16), (1 << 22, 1 << 16), "v")(arrived)
    return tendency, picked.T


def solution(mesh):
    return jax.shard_map(
        local,
        mesh=mesh,
        in_specs=(P(None, "lev", "col"), P(), P(), P(), P(), P(), P("col"), P("col")),
        out_specs=(P(None, "lev", "col"), P(None, ("col", "lev"))),
        check_vma=False,
    )
```

```python
import functools

import jax
import jax.numpy as jnp
from jax import lax
from jax.experimental import pallas as pl
from jax.experimental.pallas import tpu as pltpu
from jax.sharding import PartitionSpec as P

F32 = jnp.float32
BF16 = jnp.bfloat16
DARK = 2.0**100
GROUP = 4
WIDE = 384
PIECES = 2
HEAD = 26


def matmul(a, b, contract=((1,), (0,))):
    return lax.dot_general(a, b, (contract, ((), ())), preferred_element_type=F32)


def iota(shape, dim):
    return lax.broadcasted_iota(jnp.int32, shape, dim)


def onehot(mask):
    return jnp.where(mask, 1.0, 0.0).astype(BF16)


def per_column(row, blocks, block_cols):
    cols = blocks * block_cols
    spread = onehot(iota((blocks, cols), 1) // block_cols == iota((blocks, cols), 0))
    rows = jnp.broadcast_to(row.astype(F32), (16, blocks)).astype(BF16)
    return matmul(rows, spread)


def pack_kernel(state_hbm, phys_hbm, lit_hbm, out_hbm, data, phys_row, lit_row, packed, sems):
    fields, part, cols = state_hbm.shape
    blocks = phys_row.shape[1]
    block_cols = cols // blocks
    slots = blocks // GROUP
    copies = [
        pltpu.make_async_copy(phys_hbm, phys_row, sems.at[0]),
        pltpu.make_async_copy(lit_hbm, lit_row, sems.at[1]),
        pltpu.make_async_copy(state_hbm, data.at[:fields], sems.at[2]),
    ]
    for copy in copies:
        copy.start()
    spread = onehot(iota((blocks, cols), 1) // block_cols == iota((blocks, cols), 0))
    column = iota((1, cols), 1) % block_cols
    copies[0].wait()
    copies[1].wait()
    both = jnp.where(iota((16, blocks), 0) == 0, phys_row[...], lit_row[...])
    both = matmul(both.astype(F32).astype(BF16), spread)
    dest = both[0:1].astype(jnp.int32)
    place = ((dest % GROUP) * block_cols + column) * slots + dest // GROUP
    data[fields:] = jnp.broadcast_to(both[1:2], (2, part, cols)).astype(BF16)
    piece = cols // PIECES
    sorts = [onehot(iota((piece, cols), 0) + c * piece == place) for c in range(PIECES)]
    copies[2].wait()
    flat = data[...].reshape(WIDE, cols)
    writes = []
    for c, sort in enumerate(sorts):
        rows_c = pl.ds(c * piece, piece)
        packed[rows_c] = matmul(sort, flat, ((1,), (1,))).astype(BF16)
        writes.append(pltpu.make_async_copy(packed.at[rows_c], out_hbm.at[rows_c], sems.at[3 + c]))
        writes[-1].start()
    for write in writes:
        write.wait()


def heat_kernel(got_ref, win_ref, wout_ref, out_ref):
    pieces, slots, _ = got_ref.shape
    levs = pieces // GROUP
    fields, levels, neurons = win_ref.shape
    part = levels // levs
    count = GROUP * slots
    total = None
    for lev in range(levs):
        cols = jnp.concatenate([got_ref[g * levs + lev] for g in range(GROUP)], axis=0)
        weight = win_ref[:, lev * part : (lev + 1) * part, :].reshape(fields * part, neurons)
        term = matmul(cols[:, : fields * part], weight)
        total = term if total is None else total + term
    lit = cols[:, fields * part : fields * part + 1].astype(F32)
    heat = matmul(jnp.tanh(total).astype(BF16), wout_ref[...])
    sent = jnp.where(lit > 0.5, heat, DARK).astype(BF16)
    row = iota((count, count), 0)
    slot = (row // GROUP + HEAD) % slots
    order = onehot(iota((count, count), 1) == (row % GROUP) * slots + slot)
    out_ref[...] = matmul(order, sent).astype(BF16)


def pick_kernel(got_ref, out_ref):
    sources, levels = got_ref.shape
    row, col = iota((sources, sources), 0), iota((sources, sources), 1)
    picks = out_ref.shape[0]
    got = got_ref[...]
    lit_col = jnp.where(got[:, :1].astype(F32) < 0.5 * DARK, 1.0, 0.0)
    turn = sources - HEAD * GROUP
    place = [jnp.where(i < turn, i + HEAD * GROUP, i - turn) for i in (row, col)]
    below = onehot(place[1] < place[0])
    rank = matmul(below, jnp.broadcast_to(lit_col, (sources, picks)).astype(BF16))
    choose = jnp.where(rank == iota((sources, picks), 1).astype(F32), lit_col, 0.0).astype(BF16)
    out_ref[...] = matmul(choose, got, ((0,), (0,))).astype(BF16)


def tendency_kernel(
    lev_ref, x0, x1, x2, x3, coupling_hbm, gin, gout_hbm, sin, sout, lit_hbm, out_hbm,
    whole, coupling, gout, lit_row, terms, drag, out, sems,
):
    fields, levels, cols = whole.shape
    part = out.shape[1]
    levs = levels // part
    blocks = lit_row.shape[1]
    lev = lev_ref[0]
    copies = []
    for step, shard in enumerate((x0, x1, x2, x3)):
        source = pl.multiple_of((lev ^ step) * part, part)
        copies.append(
            pltpu.make_async_copy(shard, whole.at[:, pl.ds(source, part), :], sems.at[step])
        )
    for source, target in (
        (coupling_hbm, coupling), (gout_hbm, gout), (lit_hbm, lit_row),
    ):
        copies.append(pltpu.make_async_copy(source, target, sems.at[len(copies)]))
    for copy in copies:
        copy.start()
    own = pl.multiple_of(lev * part, part)
    for copy in copies[: levs + 1]:
        copy.wait()
    for field in range(fields):
        term = matmul(coupling[field, pl.ds(own, part), :], whole[field])
        if field < 3:
            terms[field] = term
        else:
            out[field] = term.astype(BF16)
    first = pltpu.make_async_copy(out.at[3:], out_hbm.at[3:], sems.at[len(copies)])
    first.start()
    flat = whole[...].reshape(fields * levels, cols)
    hidden = jnp.tanh(matmul(flat, gin[...], ((0,), (0,)))).astype(BF16)
    copies[levs + 1].wait()
    drag[: 2 * levels] = matmul(gout[...], hidden, ((0,), (1,)))
    hidden = jnp.tanh(matmul(flat, sin[...], ((0,), (0,)))).astype(BF16)
    copies[levs + 2].wait()
    lit = per_column(lit_row[...], blocks, cols // blocks)[0:1]
    drag[2 * levels :] = matmul(sout[...], hidden, ((0,), (1,))) * lit
    for field in range(3):
        added = drag[pl.ds(field * levels + own, part), :]
        out[field] = (terms[field] + added).astype(BF16)
    last = pltpu.make_async_copy(out.at[:3], out_hbm.at[:3], sems.at[len(copies) + 1])
    last.start()
    first.wait()
    last.wait()


def call(kernel, out, cost, spaces, scratch=(), vmem=24, result="v"):
    kinds = {"s": pltpu.SMEM, "v": pltpu.VMEM, "h": pltpu.HBM}
    return pl.pallas_call(
        kernel,
        out_shape=jax.ShapeDtypeStruct(*out),
        in_specs=[pl.BlockSpec(memory_space=kinds[space]) for space in spaces],
        out_specs=pl.BlockSpec(memory_space=kinds[result]),
        scratch_shapes=list(scratch),
        cost_estimate=pl.CostEstimate(flops=cost[0], bytes_accessed=cost[1], transcendentals=0),
        compiler_params=pltpu.CompilerParams(vmem_limit_bytes=int(vmem * 1024) << 10),
    )


def local(state, level_coupling, gwd_in, gwd_out, sw_in, sw_out, phys_device, sunlit):
    fields, part, cols = state.shape
    blocks = phys_device.shape[0]
    levs = lax.axis_size("lev")
    col_count = lax.axis_size("col")
    levels = part * levs
    slots = blocks // GROUP
    members = GROUP * levs
    phys_row = phys_device.reshape(1, blocks)
    lit_row = sunlit.reshape(1, blocks)

    keep = functools.partial(pltpu.with_memory_space_constraint, memory_space=pltpu.HBM)
    packed = call(
        pack_kernel, ((cols, WIDE), BF16), (2 * cols * cols * WIDE, 1 << 20), "hhh",
        [
            pltpu.VMEM((fields + 2, part, cols), BF16),
            pltpu.VMEM((1, blocks), jnp.int32),
            pltpu.VMEM((1, blocks), jnp.int32),
            pltpu.VMEM((cols, WIDE), BF16),
            pltpu.SemaphoreType.DMA((3 + PIECES,)),
        ],
        24, "h",
    )(keep(state), keep(phys_row), keep(lit_row)).reshape(members, slots, WIDE)
    near = [[e * members + i for i in range(members)] for e in range(col_count // GROUP)]
    got = lax.all_to_all(packed, ("col", "lev"), 0, 0, tiled=True, axis_index_groups=near)

    ring = [[(i, i ^ step) for i in range(levs)] for step in range(levs)]
    shards = [state] + [lax.ppermute(state, "lev", ring[step]) for step in range(1, levs)]

    heat = call(
        heat_kernel, ((slots * GROUP, levels), BF16),
        (2 * blocks * (fields * levels * 512 + 512 * levels), 2 << 20), "vvv",
    )(got, sw_in.reshape(fields, levels, -1), sw_out)
    far = [[(e + HEAD) % slots * GROUP + g for e in range(slots)] for g in range(GROUP)]
    arrived = lax.all_to_all(
        heat.reshape(slots, GROUP, levels), "col", 0, 0, tiled=True, axis_index_groups=far
    ).reshape(col_count, levels)

    lev = lax.axis_index("lev").astype(jnp.int32).reshape(1)
    tendency = call(
        tendency_kernel, ((fields, part, cols), BF16),
        (2 * cols * (fields * levels * 1024 + 512 * 3 * levels), 5 << 20), "shhhhhvhvvh",
        [
            pltpu.VMEM((fields, levels, cols), BF16),
            pltpu.VMEM(level_coupling.shape, BF16),
            pltpu.VMEM(gwd_out.shape, BF16),
            pltpu.VMEM((1, blocks), jnp.int32),
            pltpu.VMEM((3, part, cols), F32),
            pltpu.VMEM((3 * levels, cols), F32),
            pltpu.VMEM((fields, part, cols), BF16),
            pltpu.SemaphoreType.DMA((levs + 8,)),
        ],
        40, "h",
    )(lev, *shards, keep(level_coupling), gwd_in, keep(gwd_out), sw_in, sw_out, keep(lit_row))

    picked = call(pick_kernel, ((blocks // 2, levels), BF16), (1 << 22, 1 << 16), "v")(arrived)
    return tendency, picked.T


def solution(mesh):
    return jax.shard_map(
        local,
        mesh=mesh,
        in_specs=(P(None, "lev", "col"), P(), P(), P(), P(), P(), P("col"), P("col")),
        out_specs=(P(None, "lev", "col"), P(None, ("col", "lev"))),
        check_vma=False,
    )
```

```python
import functools

import jax
import jax.numpy as jnp
from jax import lax
from jax.experimental import pallas as pl
from jax.experimental.pallas import tpu as pltpu
from jax.sharding import PartitionSpec as P

F32 = jnp.float32
BF16 = jnp.bfloat16
DARK = 2.0**100
GROUP = 4
WIDE = 384
PIECES = 2
HEAD = 26


def matmul(a, b, contract=((1,), (0,))):
    return lax.dot_general(a, b, (contract, ((), ())), preferred_element_type=F32)


def iota(shape, dim):
    return lax.broadcasted_iota(jnp.int32, shape, dim)


def onehot(mask):
    return jnp.where(mask, 1.0, 0.0).astype(BF16)


def per_column(row, blocks, block_cols):
    cols = blocks * block_cols
    spread = onehot(iota((blocks, cols), 1) // block_cols == iota((blocks, cols), 0))
    rows = jnp.broadcast_to(row.astype(F32), (16, blocks)).astype(BF16)
    return matmul(rows, spread)


def pack_kernel(state_hbm, phys_hbm, lit_hbm, out_hbm, data, phys_row, lit_row, packed, sems):
    fields, part, cols = state_hbm.shape
    blocks = phys_row.shape[1]
    block_cols = cols // blocks
    slots = blocks // GROUP
    copies = [
        pltpu.make_async_copy(phys_hbm, phys_row, sems.at[0]),
        pltpu.make_async_copy(lit_hbm, lit_row, sems.at[1]),
        pltpu.make_async_copy(state_hbm, data.at[:fields], sems.at[2]),
    ]
    for copy in copies:
        copy.start()
    spread = onehot(iota((blocks, cols), 1) // block_cols == iota((blocks, cols), 0))
    column = iota((1, cols), 1) % block_cols
    copies[0].wait()
    copies[1].wait()
    both = jnp.where(iota((16, blocks), 0) == 0, phys_row[...], lit_row[...])
    both = matmul(both.astype(F32).astype(BF16), spread)
    dest = both[0:1].astype(jnp.int32)
    place = ((dest % GROUP) * block_cols + column) * slots + dest // GROUP
    data[fields:] = jnp.broadcast_to(both[1:2], (2, part, cols)).astype(BF16)
    piece = cols // PIECES
    sorts = [onehot(iota((piece, cols), 0) + c * piece == place) for c in range(PIECES)]
    copies[2].wait()
    flat = data[...].reshape(WIDE, cols)
    writes = []
    for c, sort in enumerate(sorts):
        rows_c = pl.ds(c * piece, piece)
        packed[rows_c] = matmul(sort, flat, ((1,), (1,))).astype(BF16)
        writes.append(pltpu.make_async_copy(packed.at[rows_c], out_hbm.at[rows_c], sems.at[3 + c]))
        writes[-1].start()
    for write in writes:
        write.wait()


def heat_kernel(got_ref, win_ref, wout_ref, out_ref):
    pieces, slots, _ = got_ref.shape
    levs = pieces // GROUP
    fields, levels, neurons = win_ref.shape
    part = levels // levs
    count = GROUP * slots
    total = None
    for lev in range(levs):
        cols = jnp.concatenate([got_ref[g * levs + lev] for g in range(GROUP)], axis=0)
        weight = win_ref[:, lev * part : (lev + 1) * part, :].reshape(fields * part, neurons)
        term = matmul(cols[:, : fields * part], weight)
        total = term if total is None else total + term
    lit = cols[:, fields * part : fields * part + 1].astype(F32)
    heat = matmul(jnp.tanh(total).astype(BF16), wout_ref[...])
    sent = jnp.where(lit > 0.5, heat, DARK).astype(BF16)
    row = iota((count, count), 0)
    slot = (row // GROUP + HEAD) % slots
    order = onehot(iota((count, count), 1) == (row % GROUP) * slots + slot)
    out_ref[...] = matmul(order, sent).astype(BF16)


def pick_kernel(got_ref, out_ref):
    sources, levels = got_ref.shape
    row, col = iota((sources, sources), 0), iota((sources, sources), 1)
    picks = out_ref.shape[0]
    got = got_ref[...].astype(F32)
    lit = got < 0.5 * DARK
    heat = jnp.where(lit, got, 0.0).astype(BF16)
    lit_col = jnp.where(lit[:, :1], 1.0, 0.0)
    turn = sources - HEAD * GROUP
    place = [jnp.where(i < turn, i + HEAD * GROUP, i - turn) for i in (row, col)]
    below = onehot(place[1] < place[0])
    rank = matmul(below, jnp.broadcast_to(lit_col, (sources, picks)).astype(BF16))
    choose = jnp.where(rank == iota((sources, picks), 1).astype(F32), lit_col, 0.0).astype(BF16)
    out_ref[...] = matmul(choose, heat, ((0,), (0,))).astype(BF16)


def tendency_kernel(
    lev_ref, x0, x1, x2, x3, coupling_hbm, gin, gout_hbm, sin, sout, lit_hbm, out_hbm,
    whole, coupling, gout, lit_row, terms, drag, out, sems,
):
    fields, levels, cols = whole.shape
    part = out.shape[1]
    levs = levels // part
    blocks = lit_row.shape[1]
    lev = lev_ref[0]
    copies = []
    for step, shard in enumerate((x0, x1, x2, x3)):
        source = pl.multiple_of((lev ^ step) * part, part)
        copies.append(
            pltpu.make_async_copy(shard, whole.at[:, pl.ds(source, part), :], sems.at[step])
        )
    for source, target in (
        (coupling_hbm, coupling), (gout_hbm, gout), (lit_hbm, lit_row),
    ):
        copies.append(pltpu.make_async_copy(source, target, sems.at[len(copies)]))
    for copy in copies:
        copy.start()
    own = pl.multiple_of(lev * part, part)
    for copy in copies[:levs]:
        copy.wait()
    flat = whole[...].reshape(fields * levels, cols)
    hidden = jnp.tanh(matmul(flat, gin[...], ((0,), (0,)))).astype(BF16)
    copies[levs].wait()
    for field in range(fields):
        term = matmul(coupling[field, pl.ds(own, part), :], whole[field])
        if field < 3:
            terms[field] = term
        else:
            out[field] = term.astype(BF16)
    first = pltpu.make_async_copy(out.at[3:], out_hbm.at[3:], sems.at[len(copies)])
    first.start()
    copies[levs + 1].wait()
    drag[: 2 * levels] = matmul(gout[...], hidden, ((0,), (1,)))
    hidden = jnp.tanh(matmul(flat, sin[...], ((0,), (0,)))).astype(BF16)
    copies[levs + 2].wait()
    lit = per_column(lit_row[...], blocks, cols // blocks)[0:1]
    drag[2 * levels :] = matmul(sout[...], hidden, ((0,), (1,))) * lit
    for field in range(3):
        added = drag[pl.ds(field * levels + own, part), :]
        out[field] = (terms[field] + added).astype(BF16)
    last = pltpu.make_async_copy(out.at[:3], out_hbm.at[:3], sems.at[len(copies) + 1])
    last.start()
    first.wait()
    last.wait()


def call(kernel, out, cost, spaces, scratch=(), vmem=24, result="v"):
    kinds = {"s": pltpu.SMEM, "v": pltpu.VMEM, "h": pltpu.HBM}
    return pl.pallas_call(
        kernel,
        out_shape=jax.ShapeDtypeStruct(*out),
        in_specs=[pl.BlockSpec(memory_space=kinds[space]) for space in spaces],
        out_specs=pl.BlockSpec(memory_space=kinds[result]),
        scratch_shapes=list(scratch),
        cost_estimate=pl.CostEstimate(flops=cost[0], bytes_accessed=cost[1], transcendentals=0),
        compiler_params=pltpu.CompilerParams(vmem_limit_bytes=int(vmem * 1024) << 10),
    )


def local(state, level_coupling, gwd_in, gwd_out, sw_in, sw_out, phys_device, sunlit):
    fields, part, cols = state.shape
    blocks = phys_device.shape[0]
    levs = lax.axis_size("lev")
    col_count = lax.axis_size("col")
    levels = part * levs
    slots = blocks // GROUP
    members = GROUP * levs
    phys_row = phys_device.reshape(1, blocks)
    lit_row = sunlit.reshape(1, blocks)

    keep = functools.partial(pltpu.with_memory_space_constraint, memory_space=pltpu.HBM)
    packed = call(
        pack_kernel, ((cols, WIDE), BF16), (2 * cols * cols * WIDE, 1 << 20), "hhh",
        [
            pltpu.VMEM((fields + 2, part, cols), BF16),
            pltpu.VMEM((1, blocks), jnp.int32),
            pltpu.VMEM((1, blocks), jnp.int32),
            pltpu.VMEM((cols, WIDE), BF16),
            pltpu.SemaphoreType.DMA((3 + PIECES,)),
        ],
        24, "h",
    )(keep(state), keep(phys_row), keep(lit_row)).reshape(members, slots, WIDE)
    near = [[e * members + i for i in range(members)] for e in range(col_count // GROUP)]
    got = lax.all_to_all(packed, ("col", "lev"), 0, 0, tiled=True, axis_index_groups=near)

    ring = [[(i, i ^ step) for i in range(levs)] for step in range(levs)]
    shards = [state] + [lax.ppermute(state, "lev", ring[step]) for step in range(1, levs)]

    heat = call(
        heat_kernel, ((slots * GROUP, levels), BF16),
        (2 * blocks * (fields * levels * 512 + 512 * levels), 2 << 20), "vvv",
    )(got, sw_in.reshape(fields, levels, -1), sw_out)
    far = [[(e + HEAD) % slots * GROUP + g for e in range(slots)] for g in range(GROUP)]
    arrived = lax.all_to_all(
        heat.reshape(slots, GROUP, levels), "col", 0, 0, tiled=True, axis_index_groups=far
    ).reshape(col_count, levels)

    lev = lax.axis_index("lev").astype(jnp.int32).reshape(1)
    tendency = call(
        tendency_kernel, ((fields, part, cols), BF16),
        (2 * cols * (fields * levels * 1024 + 512 * 3 * levels), 5 << 20), "shhhhhvhvvh",
        [
            pltpu.VMEM((fields, levels, cols), BF16),
            pltpu.VMEM(level_coupling.shape, BF16),
            pltpu.VMEM(gwd_out.shape, BF16),
            pltpu.VMEM((1, blocks), jnp.int32),
            pltpu.VMEM((3, part, cols), F32),
            pltpu.VMEM((3 * levels, cols), F32),
            pltpu.VMEM((fields, part, cols), BF16),
            pltpu.SemaphoreType.DMA((levs + 8,)),
        ],
        40, "h",
    )(lev, *shards, keep(level_coupling), gwd_in, keep(gwd_out), sw_in, sw_out, keep(lit_row))

    picked = call(pick_kernel, ((blocks // 2, levels), BF16), (1 << 22, 1 << 16), "v")(arrived)
    return tendency, picked.T


def solution(mesh):
    return jax.shard_map(
        local,
        mesh=mesh,
        in_specs=(P(None, "lev", "col"), P(), P(), P(), P(), P(), P("col"), P("col")),
        out_specs=(P(None, "lev", "col"), P(None, ("col", "lev"))),
        check_vma=False,
    )
```

```python
import functools

import jax
import jax.numpy as jnp
from jax import lax
from jax.experimental import pallas as pl
from jax.experimental.pallas import tpu as pltpu
from jax.sharding import PartitionSpec as P

F32 = jnp.float32
BF16 = jnp.bfloat16
DARK = 2.0**100
GROUP = 4
WIDE = 384
PIECES = 2
HEAD = 26


def matmul(a, b, contract=((1,), (0,))):
    return lax.dot_general(a, b, (contract, ((), ())), preferred_element_type=F32)


def iota(shape, dim):
    return lax.broadcasted_iota(jnp.int32, shape, dim)


def onehot(mask):
    return jnp.where(mask, 1.0, 0.0).astype(BF16)


def per_column(row, blocks, block_cols):
    cols = blocks * block_cols
    spread = onehot(iota((blocks, cols), 1) // block_cols == iota((blocks, cols), 0))
    rows = jnp.broadcast_to(row.astype(F32), (16, blocks)).astype(BF16)
    return matmul(rows, spread)


def pack_kernel(state_hbm, phys_hbm, lit_hbm, out_hbm, data, phys_row, lit_row, packed, sems):
    fields, part, cols = state_hbm.shape
    blocks = phys_row.shape[1]
    block_cols = cols // blocks
    slots = blocks // GROUP
    copies = [
        pltpu.make_async_copy(phys_hbm, phys_row, sems.at[0]),
        pltpu.make_async_copy(lit_hbm, lit_row, sems.at[1]),
        pltpu.make_async_copy(state_hbm, data.at[:fields], sems.at[2]),
    ]
    for copy in copies:
        copy.start()
    spread = onehot(iota((blocks, cols), 1) // block_cols == iota((blocks, cols), 0))
    column = iota((1, cols), 1) % block_cols
    copies[0].wait()
    copies[1].wait()
    both = jnp.where(iota((16, blocks), 0) == 0, phys_row[...], lit_row[...])
    both = matmul(both.astype(F32).astype(BF16), spread)
    dest = both[0:1].astype(jnp.int32)
    place = ((dest % GROUP) * block_cols + column) * slots + dest // GROUP
    data[fields:] = jnp.broadcast_to(both[1:2], (2, part, cols)).astype(BF16)
    piece = cols // PIECES
    sorts = [onehot(iota((piece, cols), 0) + c * piece == place) for c in range(PIECES)]
    copies[2].wait()
    flat = data[...].reshape(WIDE, cols)
    writes = []
    for c, sort in enumerate(sorts):
        rows_c = pl.ds(c * piece, piece)
        packed[rows_c] = matmul(sort, flat, ((1,), (1,))).astype(BF16)
        writes.append(pltpu.make_async_copy(packed.at[rows_c], out_hbm.at[rows_c], sems.at[3 + c]))
        writes[-1].start()
    for write in writes:
        write.wait()


def heat_kernel(got_ref, win_ref, wout_ref, out_ref):
    pieces, slots, _ = got_ref.shape
    levs = pieces // GROUP
    fields, levels, neurons = win_ref.shape
    part = levels // levs
    count = GROUP * slots
    total = None
    for lev in range(levs):
        cols = jnp.concatenate([got_ref[g * levs + lev] for g in range(GROUP)], axis=0)
        weight = win_ref[:, lev * part : (lev + 1) * part, :].reshape(fields * part, neurons)
        term = matmul(cols[:, : fields * part], weight)
        total = term if total is None else total + term
    lit = cols[:, fields * part : fields * part + 1].astype(F32)
    heat = matmul(jnp.tanh(total).astype(BF16), wout_ref[...])
    sent = jnp.where(lit > 0.5, heat, DARK).astype(BF16)
    row = iota((count, count), 0)
    slot = (row // GROUP + HEAD) % slots
    order = onehot(iota((count, count), 1) == (row % GROUP) * slots + slot)
    out_ref[...] = matmul(order, sent).astype(BF16)


def pick_kernel(got_ref, out_ref):
    sources, levels = got_ref.shape
    row, col = iota((sources, sources), 0), iota((sources, sources), 1)
    picks = out_ref.shape[0]
    got = got_ref[...]
    lit_col = jnp.where(got[:, :1].astype(F32) < 0.5 * DARK, 1.0, 0.0)
    turn = sources - HEAD * GROUP
    place = [jnp.where(i < turn, i + HEAD * GROUP, i - turn) for i in (row, col)]
    below = onehot(place[1] < place[0])
    rank = matmul(below, jnp.broadcast_to(lit_col, (sources, picks)).astype(BF16))
    choose = jnp.where(rank == iota((sources, picks), 1).astype(F32), lit_col, 0.0).astype(BF16)
    out_ref[...] = matmul(choose, got, ((0,), (0,))).astype(BF16)


def tendency_kernel(
    lev_ref, x0, x1, x2, x3, coupling_hbm, gin, gout_hbm, sin, sout, lit_hbm, out_hbm,
    whole, coupling, gout, lit_row, terms, drag, out, sems,
):
    fields, levels, cols = whole.shape
    part = out.shape[1]
    levs = levels // part
    blocks = lit_row.shape[1]
    lev = lev_ref[0]
    copies = []
    for step, shard in enumerate((x0, x1, x2, x3)):
        source = pl.multiple_of((lev ^ step) * part, part)
        copies.append(
            pltpu.make_async_copy(shard, whole.at[:, pl.ds(source, part), :], sems.at[step])
        )
    for source, target in (
        (coupling_hbm, coupling), (gout_hbm, gout), (lit_hbm, lit_row),
    ):
        copies.append(pltpu.make_async_copy(source, target, sems.at[len(copies)]))
    for copy in copies:
        copy.start()
    own = pl.multiple_of(lev * part, part)
    for copy in copies[:levs]:
        copy.wait()
    flat = whole[...].reshape(fields * levels, cols)
    hidden = jnp.tanh(matmul(flat, gin[...], ((0,), (0,)))).astype(BF16)
    copies[levs].wait()
    for field in range(fields):
        term = matmul(coupling[field, pl.ds(own, part), :], whole[field])
        if field < 3:
            terms[field] = term
        else:
            out[field] = term.astype(BF16)
    first = pltpu.make_async_copy(out.at[3:], out_hbm.at[3:], sems.at[len(copies)])
    first.start()
    copies[levs + 1].wait()
    drag[: 2 * levels] = matmul(gout[...], hidden, ((0,), (1,)))
    hidden = jnp.tanh(matmul(flat, sin[...], ((0,), (0,)))).astype(BF16)
    copies[levs + 2].wait()
    lit = per_column(lit_row[...], blocks, cols // blocks)[0:1]
    drag[2 * levels :] = matmul(sout[...], hidden, ((0,), (1,))) * lit
    for field in range(3):
        added = drag[pl.ds(field * levels + own, part), :]
        out[field] = (terms[field] + added).astype(BF16)
    last = pltpu.make_async_copy(out.at[:3], out_hbm.at[:3], sems.at[len(copies) + 1])
    last.start()
    first.wait()
    last.wait()


def call(kernel, out, cost, spaces, scratch=(), vmem=24, result="v"):
    kinds = {"s": pltpu.SMEM, "v": pltpu.VMEM, "h": pltpu.HBM}
    return pl.pallas_call(
        kernel,
        out_shape=jax.ShapeDtypeStruct(*out),
        in_specs=[pl.BlockSpec(memory_space=kinds[space]) for space in spaces],
        out_specs=pl.BlockSpec(memory_space=kinds[result]),
        scratch_shapes=list(scratch),
        cost_estimate=pl.CostEstimate(flops=cost[0], bytes_accessed=cost[1], transcendentals=0),
        compiler_params=pltpu.CompilerParams(vmem_limit_bytes=int(vmem * 1024) << 10),
    )


def local(state, level_coupling, gwd_in, gwd_out, sw_in, sw_out, phys_device, sunlit):
    fields, part, cols = state.shape
    blocks = phys_device.shape[0]
    levs = lax.axis_size("lev")
    col_count = lax.axis_size("col")
    levels = part * levs
    slots = blocks // GROUP
    members = GROUP * levs
    phys_row = phys_device.reshape(1, blocks)
    lit_row = sunlit.reshape(1, blocks)

    keep = functools.partial(pltpu.with_memory_space_constraint, memory_space=pltpu.HBM)
    packed = call(
        pack_kernel, ((cols, WIDE), BF16), (2 * cols * cols * WIDE, 1 << 20), "hhh",
        [
            pltpu.VMEM((fields + 2, part, cols), BF16),
            pltpu.VMEM((1, blocks), jnp.int32),
            pltpu.VMEM((1, blocks), jnp.int32),
            pltpu.VMEM((cols, WIDE), BF16),
            pltpu.SemaphoreType.DMA((3 + PIECES,)),
        ],
        24, "h",
    )(keep(state), keep(phys_row), keep(lit_row)).reshape(members, slots, WIDE)
    near = [[e * members + i for i in range(members)] for e in range(col_count // GROUP)]
    got = lax.all_to_all(packed, ("col", "lev"), 0, 0, tiled=True, axis_index_groups=near)

    ring = [[(i, i ^ step) for i in range(levs)] for step in range(levs)]
    shards = [state] + [lax.ppermute(state, "lev", ring[step]) for step in range(1, levs)]

    heat = call(
        heat_kernel, ((slots * GROUP, levels), BF16),
        (2 * blocks * (fields * levels * 512 + 512 * levels), 2 << 20), "vvv",
    )(got, sw_in.reshape(fields, levels, -1), sw_out)
    far = [[(e + HEAD) % slots * GROUP + g for e in range(slots)] for g in range(GROUP)]
    arrived = lax.all_to_all(
        heat.reshape(slots, GROUP, levels), "col", 0, 0, tiled=True, axis_index_groups=far
    ).reshape(col_count, levels)

    lev = lax.axis_index("lev").astype(jnp.int32).reshape(1)
    tendency = call(
        tendency_kernel, ((fields, part, cols), BF16),
        (2 * cols * (fields * levels * 1024 + 512 * 3 * levels), 5 << 20), "shhhhhvhvvh",
        [
            pltpu.VMEM((fields, levels, cols), BF16),
            pltpu.VMEM(level_coupling.shape, BF16),
            pltpu.VMEM(gwd_out.shape, BF16),
            pltpu.VMEM((1, blocks), jnp.int32),
            pltpu.VMEM((3, part, cols), F32),
            pltpu.VMEM((3 * levels, cols), F32),
            pltpu.VMEM((fields, part, cols), BF16),
            pltpu.SemaphoreType.DMA((levs + 8,)),
        ],
        40, "h",
    )(lev, *shards, keep(level_coupling), gwd_in, keep(gwd_out), sw_in, sw_out, keep(lit_row))

    picked = call(pick_kernel, ((blocks // 2, levels), BF16), (1 << 22, 1 << 16), "v")(arrived)
    return tendency, picked.T


def solution(mesh):
    return jax.shard_map(
        local,
        mesh=mesh,
        in_specs=(P(None, "lev", "col"), P(), P(), P(), P(), P(), P("col"), P("col")),
        out_specs=(P(None, "lev", "col"), P(None, ("col", "lev"))),
        check_vma=False,
    )
```
